256 devices in a mesh: dp: 32 (over x, y, z_lo), ctx: 8 (over z_hi, core).
Axes of the slice: x: 4, y: 4, z: 8 (z_hi: 4, z_lo: 2; z = z_hi * 2 + z_lo), core: 2. Of those that a mesh axis runs over, the one named last changes fastest.
Arguments:
- queries: bfloat16 [32, 512, 3072], P('dp', 'ctx'), may hold values from -6 to 6
- keys: bfloat16 [32, 1024, 3072], P('dp', 'ctx'), may hold values from -6 to 6
- values: bfloat16 [32, 1024, 3072], P('dp', 'ctx'), may hold values from -6 to 6
- tan_q: bfloat16 [32, 512, 3072], P('dp', 'ctx'), may hold values from -6 to 6
- tan_k: bfloat16 [32, 1024, 3072], P('dp', 'ctx'), may hold values from -6 to 6
- tan_v: bfloat16 [32, 1024, 3072], P('dp', 'ctx'), may hold values from -6 to 6
- attn_cot: bfloat16 [32, 512, 3072], P('dp', 'ctx'), may hold values from -6 to 6
- out_cot: bfloat16 [32, 512, 6144], P('dp', 'ctx'), may hold values from -6 to 6
Outputs:
- grad_q: bfloat16 [32, 512, 3072], P('dp', 'ctx')
- grad_k: bfloat16 [32, 1024, 3072], P('dp', 'ctx')
- grad_v: bfloat16 [32, 1024, 3072], P('dp', 'ctx')
- grad_weight: float32 [3072, 6144], P(('ctx', 'dp'))
The draws below stay inside these ranges and needn't reach their ends.
All inputs are finite; a program needn't handle non-finite values.
Results may differ from the reference program's by a relative error of at most 0.015.
Values may be sent and summed in bfloat16 or wider, within the bound.
No kernel may reach another device: no remote copies, remote signals or barrier semaphores. Data moves between devices by JAX's collectives and lax.ppermute only.
A program may use at most 128 MiB of HBM per device.

```python
import jax
import jax.numpy as jnp
from jax import lax

D = 6144
H = 24
E = 128
BATCH = 32
SLAB = 512
SEQ = 1024


def draw_queries(key, part):
    key = jax.random.fold_in(key, 3)
    result = jnp.clip(jax.random.normal(key, (BATCH, SLAB, H * E), jnp.float32), -6.0, 6.0)
    return result.astype(jnp.bfloat16)


def draw_keys(key, part):
    key = jax.random.fold_in(key, 5)
    result = jnp.clip(jax.random.normal(key, (BATCH, SEQ, H * E), jnp.float32), -6.0, 6.0)
    return result.astype(jnp.bfloat16)


def level_of(stream_key, shape, cuts, low, high):
    def one(dim, shards_of):
        draws = jax.random.uniform(jax.random.fold_in(jax.random.fold_in(stream_key, 6), dim), (shards_of,), jnp.float32, low / len(cuts), high / len(cuts))
        return jnp.repeat(jnp.exp(draws), shape[dim] // shards_of).reshape((-1,) + (1,) * (len(shape) - dim - 1))

    gain = one(*cuts[0])
    for cut in cuts[1:]:
        gain = gain * one(*cut)
    return gain


def gaussian(rng, dims, width, most, shards=(), dtype=jnp.bfloat16):
    entries = jax.random.normal(rng, dims, jnp.float32) * width
    if len(shards) > 0:
        entries = level_of(rng, dims, shards, -0.22, 0.18) * entries
    return jnp.clip(entries, min=-most, max=most).astype(dtype)


def setup_inputs(seed: int = 0) -> dict:
    key_of = jax.random.split(jax.random.key(seed), 9)
    return {
        "queries": draw_queries(jax.random.fold_in(key_of[8], 71), 0),
        "keys": draw_keys(jax.random.fold_in(key_of[8], 71), 0),
        "values": gaussian(key_of[2], (BATCH, SEQ, H * E), 1.0, 6.0, ((0, 32), (1, 8))),
        "tan_q": gaussian(key_of[3], (BATCH, SLAB, H * E), 1.0, 6.0, ((0, 32), (1, 8))),
        "tan_k": gaussian(key_of[4], (BATCH, SEQ, H * E), 1.0, 6.0, ((0, 32), (1, 8))),
        "tan_v": gaussian(key_of[5], (BATCH, SEQ, H * E), 1.0, 6.0, ((0, 32), (1, 8))),
        "attn_cot": gaussian(key_of[6], (BATCH, SLAB, H * E), 1.0, 6.0, ((0, 32), (1, 8))),
        "out_cot": gaussian(key_of[7], (BATCH, SLAB, D), 1.0, 6.0, ((0, 32), (1, 8))),
    }


def head_pass(inputs):
    queries_h, keys_h, values_h, tangent_q, tangent_k, tangent_v, cotangent = inputs
    factor = E ** -0.5
    scores = jnp.dot(queries_h, keys_h.T, preferred_element_type=jnp.float32) * factor
    highest = jnp.max(scores, axis=-1, keepdims=True)
    weights = jnp.exp(scores - highest)
    probs = weights / jnp.sum(weights, axis=-1, keepdims=True)
    probs_low = probs.astype(jnp.bfloat16)
    out_full = jnp.dot(probs_low, values_h, preferred_element_type=jnp.float32)
    out_low = out_full.astype(jnp.bfloat16)
    tangent_scores = (jnp.dot(queries_h, tangent_k.T, preferred_element_type=jnp.float32)
                      + jnp.dot(tangent_q, keys_h.T, preferred_element_type=jnp.float32)) * factor
    mixed_full = probs * tangent_scores
    tangent_rows = jnp.sum(mixed_full, axis=-1, keepdims=True)
    mixed_low = mixed_full.astype(jnp.bfloat16)
    tangent_out = (jnp.dot(probs_low, tangent_v, preferred_element_type=jnp.float32)
                   + jnp.dot(mixed_low, values_h, preferred_element_type=jnp.float32)
                   - tangent_rows * out_full)
    grad_out = (cotangent.astype(jnp.float32) + tangent_out).astype(jnp.bfloat16)
    delta_rows = jnp.sum(grad_out.astype(jnp.float32) * out_low.astype(jnp.float32), axis=-1, keepdims=True)
    grad_probs = jnp.dot(grad_out, values_h.T, preferred_element_type=jnp.float32)
    grad_scores = (probs * (grad_probs - delta_rows)).astype(jnp.bfloat16)
    grad_query = (jnp.dot(grad_scores, keys_h, preferred_element_type=jnp.float32) * factor).astype(jnp.bfloat16)
    grad_key = (jnp.dot(grad_scores.T, queries_h, preferred_element_type=jnp.float32) * factor).astype(jnp.bfloat16)
    grad_value = jnp.dot(probs_low.T, grad_out, preferred_element_type=jnp.float32).astype(jnp.bfloat16)
    return grad_query, grad_key, grad_value, out_low


def split_heads(matrix):
    return matrix.reshape(matrix.shape[0], H, E).transpose(1, 0, 2)


def join_heads(stacked):
    return stacked.transpose(1, 0, 2).reshape(stacked.shape[1], H * E)


def reference(queries, keys, values, tan_q, tan_k, tan_v, attn_cot, out_cot):
    def clip_pass(running, inputs):
        heads = tuple(split_heads(member) for member in inputs[:7])
        results = lax.map(head_pass, heads)
        grad_query = join_heads(results[0])
        grad_key = join_heads(results[1])
        grad_value = join_heads(results[2])
        outputs_low = join_heads(results[3])
        running = running + lax.dot_general(outputs_low, inputs[7], (((0,), (0,)), ((), ())),
                                            preferred_element_type=jnp.float32)
        return running, (grad_query, grad_key, grad_value)

    initial = jnp.zeros((H * E, D), jnp.float32)
    grad_weight, grads = lax.scan(clip_pass, initial,
                                  (queries, keys, values, tan_q, tan_k, tan_v, attn_cot, out_cot))
    return grads[0], grads[1], grads[2], grad_weight
```

```python
import jax
import jax.numpy as jnp
from jax import lax
from jax.experimental import pallas as pl
from jax.experimental.pallas import tpu as pltpu
from jax.sharding import Mesh, PartitionSpec as P

E = 128
HEADS = 3
WIDTH = HEADS * E
CTX = 8
ROWS = 64
KEY_ROWS = 128
FACTOR = E ** -0.5
LOG2E = 1.4426950408889634
F32 = jnp.float32
BF16 = jnp.bfloat16
VMEM_LIMIT = 56 * 1024 * 1024

NT = (((1,), (1,)), ((), ()))
TN = (((0,), (0,)), ((), ()))


def params():
    return pltpu.CompilerParams(vmem_limit_bytes=VMEM_LIMIT)


def cost(flops, moved, exps=0):
    return pl.CostEstimate(flops=flops, bytes_accessed=moved, transcendentals=exps)


def pack_main_kernel(k_ref, v_ref, q_ref, o_ref):
    o_ref[0, 0:128] = k_ref[0]
    o_ref[0, 128:256] = v_ref[0]
    o_ref[0, 256:320] = q_ref[0]


def pack_main(keys, values, queries):
    wide = pl.BlockSpec((1, KEY_ROWS, WIDTH), lambda d: (0, 0, d))
    short = pl.BlockSpec((1, ROWS, WIDTH), lambda d: (0, 0, d))
    return pl.pallas_call(
        pack_main_kernel,
        grid=(CTX,),
        in_specs=[wide, wide, short],
        out_specs=pl.BlockSpec((1, 320, WIDTH), lambda d: (d, 0, 0)),
        out_shape=jax.ShapeDtypeStruct((CTX, 320, WIDTH), BF16),
        compiler_params=params(),
        cost_estimate=cost(0, 4 << 20),
    )(keys, values, queries)


def pack_tangent_kernel(tk_ref, tv_ref, tq_ref, cot_ref, *outs):
    for h in range(HEADS):
        lanes = slice(h * E, (h + 1) * E)
        outs[h][0, 0:128] = tk_ref[0, :, lanes]
        outs[h][0, 128:256] = tv_ref[0, :, lanes]
        outs[h][0, 256:320] = tq_ref[0, :, lanes]
        outs[h][0, 320:384] = cot_ref[0, :, lanes]


def pack_tangents(tan_k, tan_v, tan_q, attn_cot):
    wide = pl.BlockSpec((1, KEY_ROWS, WIDTH), lambda d: (0, 0, d))
    short = pl.BlockSpec((1, ROWS, WIDTH), lambda d: (0, 0, d))
    return pl.pallas_call(
        pack_tangent_kernel,
        grid=(CTX,),
        in_specs=[wide, wide, short, short],
        out_specs=[pl.BlockSpec((1, 384, E), lambda d: (d, 0, 0))] * HEADS,
        out_shape=[jax.ShapeDtypeStruct((CTX, 384, E), BF16)] * HEADS,
        compiler_params=params(),
        cost_estimate=cost(0, 5 << 20),
    )(tan_k, tan_v, tan_q, attn_cot)


def pack_cot_kernel(c_ref, o_ref):
    o_ref[...] = c_ref[...]


def pack_cot(out_cot):
    return pl.pallas_call(
        pack_cot_kernel,
        grid=(4,),
        in_specs=[pl.BlockSpec((1, ROWS, 1536), lambda d: (0, 0, d))],
        out_specs=pl.BlockSpec((1, ROWS, 1536), lambda d: (d, 0, 0)),
        out_shape=jax.ShapeDtypeStruct((4, ROWS, 1536), BF16),
        compiler_params=params(),
        cost_estimate=cost(0, 1600000),
    )(out_cot)


def probabilities(q, k):
    s = lax.dot_general(q, k, NT, preferred_element_type=F32)
    highest = jnp.max(s, axis=-1, keepdims=True)
    w = jnp.exp2((s - highest) * (FACTOR * LOG2E))
    return w * (1.0 / jnp.sum(w, axis=-1, keepdims=True))


def forward_kernel(k_ref, v_ref, q_ref, o_ref):
    for h in range(HEADS):
        lanes = slice(h * E, (h + 1) * E)
        k = k_ref[:, :, lanes].reshape(1024, E)
        v = v_ref[:, :, lanes].reshape(1024, E)
        for part in range(2):
            q = q_ref[4 * part:4 * part + 4, :, lanes].reshape(256, E)
            p = probabilities(q, k).astype(BF16)
            o = jnp.dot(p, v, preferred_element_type=F32)
            turned = o.T.astype(BF16)
            f = 0
            while f < E:
                g = h * E + f
                slot, row = g // 96, g % 96
                n = min(E - f, 96 - row)
                for t in range(2):
                    o_ref[slot * 4 + part * 2 + t, row:row + n, :] = turned[f:f + n, t * 128:(t + 1) * 128]
                f += n


def forward(packed):
    return pl.pallas_call(
        forward_kernel,
        grid=(1,),
        in_specs=[
            pl.BlockSpec((CTX, 128, WIDTH), lambda i: (0, 0, 0)),
            pl.BlockSpec((CTX, 128, WIDTH), lambda i: (0, 1, 0)),
            pl.BlockSpec((CTX, 64, WIDTH), lambda i: (0, 4, 0)),
        ],
        out_specs=pl.BlockSpec((16, 96, 128), lambda i: (0, 0, 0)),
        out_shape=jax.ShapeDtypeStruct((16, 96, 128), BF16),
        compiler_params=params(),
        cost_estimate=cost(3 * 2 * 2 * 512 * 1024 * 128, 3 << 20, 3 * 512 * 1024),
    )(packed, packed, packed)


def backward_kernel(k_ref, v_ref, q_ref, t_ref, o_ref, gk_ref, gv_ref):
    k = k_ref[...].reshape(1024, E)
    v = v_ref[...].reshape(1024, E)
    tk = t_ref[:, 0:128].reshape(1024, E)
    tv = t_ref[:, 128:256].reshape(1024, E)
    tk_k = jnp.concatenate([tk, k], axis=1)
    v_tv = jnp.concatenate([v, tv], axis=1)
    for part in range(2):
        own = slice(4 * part, 4 * part + 4)
        q = q_ref[own].reshape(256, E)
        tq = t_ref[own, 256:320].reshape(256, E)
        cot = t_ref[own, 320:384].reshape(256, E).astype(F32)
        p = probabilities(q, k)
        p_low = p.astype(BF16)
        mixed = p * lax.dot_general(
            jnp.concatenate([q, tq], axis=1), tk_k, NT, preferred_element_type=F32
        )
        rows = jnp.sum(mixed, axis=-1, keepdims=True)
        both = jnp.dot(p_low, v_tv, preferred_element_type=F32)
        out_full = both[:, :E]
        tangent = both[:, E:] + FACTOR * (
            jnp.dot(mixed.astype(BF16), v, preferred_element_type=F32) - rows * out_full
        )
        grad_out = (cot + tangent).astype(BF16)
        delta = jnp.sum(
            grad_out.astype(F32) * out_full.astype(BF16).astype(F32), axis=-1, keepdims=True
        )
        grad_probs = lax.dot_general(grad_out, v, NT, preferred_element_type=F32)
        grad_scores = (p * (grad_probs - delta)).astype(BF16)
        grad_q = jnp.dot(grad_scores, k, preferred_element_type=F32) * FACTOR
        o_ref[own, 256:320] = grad_q.astype(BF16).reshape(4, ROWS, E)
        grad_k = lax.dot_general(q, grad_scores, TN, preferred_element_type=F32)
        grad_v = lax.dot_general(grad_out, p_low, TN, preferred_element_type=F32)
        if part == 0:
            gk_ref[...] = grad_k
            gv_ref[...] = grad_v
        else:
            grad_k = gk_ref[...] + grad_k
            grad_v = gv_ref[...] + grad_v
            o_ref[:, 0:128] = (grad_k * FACTOR).T.astype(BF16).reshape(CTX, 128, E)
            o_ref[:, 128:256] = grad_v.T.astype(BF16).reshape(CTX, 128, E)


def backward(packed, tangents, head):
    return pl.pallas_call(
        backward_kernel,
        grid=(1,),
        in_specs=[
            pl.BlockSpec((CTX, 128, E), lambda i: (0, 0, head)),
            pl.BlockSpec((CTX, 128, E), lambda i: (0, 1, head)),
            pl.BlockSpec((CTX, 64, E), lambda i: (0, 4, head)),
            pl.BlockSpec((CTX, 384, E), lambda i: (0, 0, 0)),
        ],
        out_specs=pl.BlockSpec((CTX, 320, E), lambda i: (0, 0, 0)),
        out_shape=jax.ShapeDtypeStruct((CTX, 320, E), BF16),
        scratch_shapes=[pltpu.VMEM((E, 1024), F32), pltpu.VMEM((E, 1024), F32)],
        compiler_params=params(),
        cost_estimate=cost(10 * 2 * 512 * 1024 * 128, 2 << 20, 512 * 1024),
    )(packed, packed, packed, tangents)


def unpack_kernel(*refs):
    ins, (gk_ref, gv_ref, gq_ref) = refs[:HEADS], refs[HEADS:]
    for h in range(HEADS):
        lanes = slice(h * E, (h + 1) * E)
        gk_ref[0, :, lanes] = ins[h][0, 0:128]
        gv_ref[0, :, lanes] = ins[h][0, 128:256]
        gq_ref[0, :, lanes] = ins[h][0, 256:320]


def unpack(parts):
    wide = pl.BlockSpec((1, KEY_ROWS, WIDTH), lambda d: (0, 0, d))
    short = pl.BlockSpec((1, ROWS, WIDTH), lambda d: (0, 0, d))
    return pl.pallas_call(
        unpack_kernel,
        grid=(CTX,),
        in_specs=[pl.BlockSpec((1, 320, E), lambda d: (d, 0, 0))] * HEADS,
        out_specs=[wide, wide, short],
        out_shape=[
            jax.ShapeDtypeStruct((1, KEY_ROWS, CTX * WIDTH), BF16),
            jax.ShapeDtypeStruct((1, KEY_ROWS, CTX * WIDTH), BF16),
            jax.ShapeDtypeStruct((1, ROWS, CTX * WIDTH), BF16),
        ],
        compiler_params=params(),
        cost_estimate=cost(0, 4 << 20),
    )(*parts)


def weight_kernel(a_ref, b_ref, o_ref, acc_ref, out_ref):
    step = pl.program_id(0)
    a = jnp.concatenate([a_ref[4 * x:4 * x + 4].reshape(384, 128) for x in range(4)], axis=1)
    product = jnp.dot(a, b_ref[...].reshape(512, 1536), preferred_element_type=F32)

    @pl.when(step == 0)
    def _():
        acc_ref[...] = product

    @pl.when(step > 0)
    def _():
        acc_ref[...] += product

    @pl.when(step == 3)
    def _():
        for zh in range(4):
            for yz in range(8):
                row = zh * 96 + yz * 12
                for j in range(12):
                    out_ref[yz * 4 + zh, 12 * j:12 * j + 12, :] = acc_ref[row:row + 12, 128 * j:128 * (j + 1)]
        o_ref[...] = out_ref[...].astype(BF16)


def weight_partial(a, b):
    return pl.pallas_call(
        weight_kernel,
        grid=(4,),
        in_specs=[
            pl.BlockSpec((16, 96, 128), lambda y: (y, 0, 0)),
            pl.BlockSpec((8, 1, ROWS, 1536), lambda y: (0, y, 0, 0)),
        ],
        out_specs=pl.BlockSpec((32, 144, 128), lambda y: (0, 0, 0)),
        out_shape=jax.ShapeDtypeStruct((32, 144, 128), BF16),
        scratch_shapes=[pltpu.VMEM((384, 1536), F32), pltpu.VMEM((32, 144, 128), F32)],
        compiler_params=params(),
        cost_estimate=cost(2 * 384 * 2048 * 1536, 9 << 20),
    )(a, b)


def total_kernel(r_ref, o_ref, sum_ref):
    for y in range(4):
        total = r_ref[8 * y].astype(F32)
        for z in range(1, 8):
            total = total + r_ref[8 * y + z].astype(F32)
        sum_ref[y] = total
        for j in range(12):
            lane = (12 * y + j) * 128
            o_ref[:, lane:lane + 128] = sum_ref[y, 12 * j:12 * j + 12, :]


def weight_total(received):
    return pl.pallas_call(
        total_kernel,
        out_shape=jax.ShapeDtypeStruct((12, 6144), F32),
        scratch_shapes=[pltpu.VMEM((4, 144, 128), F32)],
        compiler_params=params(),
        cost_estimate=cost(1 << 20, 2 << 20),
    )(received)


def exchange(blocks, axes):
    return lax.all_to_all(blocks, axes, split_axis=0, concat_axis=0, tiled=True)


def on_device(queries, keys, values, tan_q, tan_k, tan_v, attn_cot, out_cot):
    packed = exchange(pack_main(keys, values, queries), ("zh", "core"))
    tangents = pack_tangents(tan_k, tan_v, tan_q, attn_cot)
    tangents = [exchange(t, ("zh", "core")) for t in tangents]

    cot = exchange(pack_cot(out_cot), "y")
    cot = lax.all_gather(cot.reshape(4 * ROWS, 1536), ("x", "core"), axis=0, tiled=True)

    att = exchange(forward(packed), ("x", "zh"))
    att = lax.all_gather(att, "y", axis=0, tiled=True)
    partial = weight_partial(att, cot.reshape(8, 4, ROWS, 1536))
    weight = weight_total(exchange(partial, ("y", "zl", "zh")))

    grads = [exchange(backward(packed, tangents[h], h), ("zh", "core")) for h in range(HEADS)]
    grad_k, grad_v, grad_q = unpack(grads)
    return grad_q, grad_k, grad_v, weight


def solution(mesh):
    fine = Mesh(mesh.devices.reshape(4, 4, 2, 4, 2), ("x", "y", "zl", "zh", "core"))
    clip, token = ("x", "y", "zl"), ("zh", "core")
    placed = P(clip, token, None)
    return jax.shard_map(
        on_device,
        mesh=fine,
        in_specs=(placed,) * 8,
        out_specs=(placed, placed, placed, P(token + clip, None)),
        check_vma=False,
    )
```

```python
import functools

import jax
import jax.numpy as jnp
from jax import lax
from jax.experimental import pallas as pl
from jax.experimental.pallas import tpu as pltpu
from jax.sharding import Mesh, PartitionSpec as P

E = 128
HEADS = 3
WIDTH = HEADS * E
CTX = 8
ROWS = 64
KEY_ROWS = 128
FACTOR = E ** -0.5
LOG2E = 1.4426950408889634
F32 = jnp.float32
BF16 = jnp.bfloat16
MX, MY, MZ, MC = range(4)
SWAP = [(0, 1), (1, 0)]
VMEM_LIMIT = 56 * 1024 * 1024

NT = (((1,), (1,)), ((), ()))
TN = (((0,), (0,)), ((), ()))


def params():
    return pltpu.CompilerParams(vmem_limit_bytes=VMEM_LIMIT)


def cost(flops, moved, exps=0):
    return pl.CostEstimate(flops=flops, bytes_accessed=moved, transcendentals=exps)


def scalars():
    return pl.BlockSpec(memory_space=pltpu.SMEM)


def pack_kernel(*refs):
    o_ref = refs[-1]
    row = 0
    for ref in refs[:-1]:
        n = ref.shape[1]
        for d in range(CTX):
            o_ref[d, row:row + n] = ref[0, :, d * WIDTH:(d + 1) * WIDTH]
        row += n


def pack(*arrays):
    rows = sum(a.shape[1] for a in arrays)
    return pl.pallas_call(
        pack_kernel,
        out_shape=jax.ShapeDtypeStruct((CTX, rows, WIDTH), BF16),
        compiler_params=params(),
        cost_estimate=cost(0, 4 * rows * CTX * WIDTH),
    )(*arrays)


def pack_ahead_kernel(me_ref, *refs):
    ins, outs = refs[:3], refs[3:]
    for dz in range(4):
        for dc in range(2):
            o_ref = outs[4].at[dz] if dc else outs[dz]
            lane = pl.multiple_of(partner(me_ref, dz, dc) * WIDTH, 128)
            row = 0
            for ref in ins:
                n = ref.shape[1]
                o_ref[row:row + n] = ref[0, :, pl.ds(lane, WIDTH)]
                row += n


def pack_ahead(me, *arrays):
    rows = sum(a.shape[1] for a in arrays)
    return pl.pallas_call(
        pack_ahead_kernel,
        in_specs=[scalars()] + [pl.BlockSpec(memory_space=pltpu.VMEM)] * 3,
        out_shape=[jax.ShapeDtypeStruct((rows, WIDTH), BF16)] * 4 + [jax.ShapeDtypeStruct((4, rows, WIDTH), BF16)],
        compiler_params=params(),
        cost_estimate=cost(0, 4 * rows * CTX * WIDTH),
    )(me, *arrays)


def spread_cot_kernel(c_ref, o_ref):
    for x in range(4):
        for y in range(4):
            o_ref[4 * x + y] = c_ref[0, :, y * 1536:(y + 1) * 1536]


def spread_cot(out_cot):
    return pl.pallas_call(
        spread_cot_kernel,
        out_shape=jax.ShapeDtypeStruct((16, ROWS, 1536), BF16),
        compiler_params=params(),
        cost_estimate=cost(0, 4000000),
    )(out_cot)


def join_kernel(axis, me_ref, *refs):
    o_ref = refs[-1]
    for j in range(4):
        o_ref[lax.rem(me_ref[axis] + 4 - j, 4)] = refs[j][...]


def join(me, axis, parts):
    return pl.pallas_call(
        functools.partial(join_kernel, axis),
        in_specs=[scalars()] + [pl.BlockSpec(memory_space=pltpu.VMEM)] * 4,
        out_shape=jax.ShapeDtypeStruct((4,) + parts[0].shape, BF16),
        compiler_params=params(),
        cost_estimate=cost(0, 16 * parts[0].size),
    )(me, *parts)


def turn_kernel(me_ref, *refs):
    ins, outs = refs[:4], refs[4:]
    for k in range(4):
        zh = lax.rem(me_ref[MZ] + 4 - k, 4)
        for j in range(4):
            outs[j][zh] = ins[k][lax.rem(me_ref[MX] + j, 4)]


def turn(me, parts):
    return pl.pallas_call(
        turn_kernel,
        in_specs=[scalars()] + [pl.BlockSpec(memory_space=pltpu.VMEM)] * 4,
        out_shape=[jax.ShapeDtypeStruct((4, 96, 128), BF16)] * 4,
        compiler_params=params(),
        cost_estimate=cost(0, 800000),
    )(me, *parts)


def probabilities(q, k):
    s = lax.dot_general(q, k, NT, preferred_element_type=F32)
    highest = jnp.max(s, axis=-1, keepdims=True)
    w = jnp.exp2((s - highest) * (FACTOR * LOG2E))
    return w * (1.0 / jnp.sum(w, axis=-1, keepdims=True))


def forward_kernel(me_ref, *refs):
    ins, outs, (all_ref, in_ref) = refs[:CTX], refs[CTX:CTX + 4], refs[CTX + 4:]
    for r in range(CTX):
        in_ref[partner(me_ref, 4 - r // 2, r % 2)] = ins[r][...]
    for h in range(HEADS):
        lanes = slice(h * E, (h + 1) * E)
        k = in_ref[:, 0:128, lanes].reshape(1024, E)
        v = in_ref[:, 128:256, lanes].reshape(1024, E)
        for part in range(2):
            q = in_ref[4 * part:4 * part + 4, 256:320, lanes].reshape(256, E)
            p = probabilities(q, k).astype(BF16)
            o = jnp.dot(p, v, preferred_element_type=F32)
            turned = o.T.astype(BF16)
            f = 0
            while f < E:
                g = h * E + f
                slot, row = g // 96, g % 96
                n = min(E - f, 96 - row)
                for t in range(2):
                    all_ref[part * 2 + t, slot, row:row + n, :] = turned[f:f + n, t * 128:(t + 1) * 128]
                f += n
    for j in range(4):
        outs[j][...] = all_ref[lax.rem(me_ref[MZ] + j, 4)]


def forward(me, packed):
    return pl.pallas_call(
        forward_kernel,
        in_specs=[scalars()] + [pl.BlockSpec(memory_space=pltpu.VMEM)] * CTX,
        out_shape=[jax.ShapeDtypeStruct((4, 96, 128), BF16)] * 4,
        scratch_shapes=[pltpu.VMEM((4, 4, 96, 128), BF16), pltpu.VMEM((CTX, 320, WIDTH), BF16)],
        compiler_params=params(),
        cost_estimate=cost(3 * 2 * 2 * 512 * 1024 * 128, 3 << 20, 3 * 512 * 1024),
    )(me, *packed)


def backward_kernel(me_ref, tk_ref, tv_ref, tq_ref, cot_ref, *refs):
    ins, outs, (in_ref, o_ref, gk_ref, gv_ref) = refs[:CTX], refs[CTX:2 * CTX], refs[2 * CTX:]
    for r in range(CTX):
        in_ref[partner(me_ref, 4 - r // 2, r % 2)] = ins[r][...]
    k = in_ref[:, 0:128].reshape(1024, E)
    v = in_ref[:, 128:256].reshape(1024, E)
    tk = tk_ref[...].reshape(1024, E)
    tv = tv_ref[...].reshape(1024, E)
    tk_k = jnp.concatenate([tk, k], axis=1)
    v_tv = jnp.concatenate([v, tv], axis=1)
    for part in range(2):
        own = slice(4 * part, 4 * part + 4)
        q = in_ref[own, 256:320].reshape(256, E)
        tq = tq_ref[own].reshape(256, E)
        cot = cot_ref[own].reshape(256, E).astype(F32)
        p = probabilities(q, k)
        p_low = p.astype(BF16)
        mixed = p * lax.dot_general(
            jnp.concatenate([q, tq], axis=1), tk_k, NT, preferred_element_type=F32
        )
        rows = jnp.sum(mixed, axis=-1, keepdims=True)
        both = jnp.dot(p_low, v_tv, preferred_element_type=F32)
        out_full = both[:, :E]
        tangent = both[:, E:] + FACTOR * (
            jnp.dot(mixed.astype(BF16), v, preferred_element_type=F32) - rows * out_full
        )
        grad_out = (cot + tangent).astype(BF16)
        delta = jnp.sum(
            grad_out.astype(F32) * out_full.astype(BF16).astype(F32), axis=-1, keepdims=True
        )
        grad_probs = lax.dot_general(grad_out, v, NT, preferred_element_type=F32)
        grad_scores = (p * (grad_probs - delta)).astype(BF16)
        grad_q = jnp.dot(grad_scores, k, preferred_element_type=F32) * FACTOR
        o_ref[own, 256:320] = grad_q.astype(BF16).reshape(4, ROWS, E)
        grad_k = lax.dot_general(q, grad_scores, TN, preferred_element_type=F32)
        grad_v = lax.dot_general(grad_out, p_low, TN, preferred_element_type=F32)
        if part == 0:
            gk_ref[...] = grad_k
            gv_ref[...] = grad_v
        else:
            grad_k = gk_ref[...] + grad_k
            grad_v = gv_ref[...] + grad_v
            o_ref[:, 0:128] = (grad_k * FACTOR).T.astype(BF16).reshape(CTX, 128, E)
            o_ref[:, 128:256] = grad_v.T.astype(BF16).reshape(CTX, 128, E)
    for r in range(CTX):
        outs[r][...] = o_ref[partner(me_ref, r // 2, r % 2)]


def partner(me_ref, ahead, other):
    return lax.rem(me_ref[MZ] + ahead, 4) * 2 + lax.rem(me_ref[MC] + other, 2)


def backward(me, packed, tangents):
    return pl.pallas_call(
        backward_kernel,
        grid=(HEADS,),
        in_specs=[
            scalars(),
            pl.BlockSpec((CTX, 128, E), lambda h: (0, 0, h)),
            pl.BlockSpec((CTX, 128, E), lambda h: (0, 1, h)),
            pl.BlockSpec((CTX, 64, E), lambda h: (0, 4, h)),
            pl.BlockSpec((CTX, 64, E), lambda h: (0, 5, h)),
        ]
        + [pl.BlockSpec((320, E), lambda h: (0, h))] * CTX,
        out_specs=[pl.BlockSpec((320, E), lambda h: (0, h))] * CTX,
        out_shape=[jax.ShapeDtypeStruct((320, WIDTH), BF16)] * CTX,
        scratch_shapes=[
            pltpu.VMEM((CTX, 320, E), BF16),
            pltpu.VMEM((CTX, 320, E), BF16),
            pltpu.VMEM((E, 1024), F32),
            pltpu.VMEM((E, 1024), F32),
        ],
        compiler_params=params(),
        cost_estimate=cost(3 * 10 * 2 * 512 * 1024 * 128, 6 << 20, 3 * 512 * 1024),
    )(me, tangents, tangents, tangents, tangents, *packed)


def unpack_kernel(me_ref, *refs):
    ins, (gk_ref, gv_ref, gq_ref) = refs[:CTX], refs[CTX:]
    for r in range(CTX):
        lane = pl.multiple_of(partner(me_ref, 4 - r // 2, r % 2) * WIDTH, 128)
        gk_ref[0, :, pl.ds(lane, WIDTH)] = ins[r][0:128]
        gv_ref[0, :, pl.ds(lane, WIDTH)] = ins[r][128:256]
        gq_ref[0, :, pl.ds(lane, WIDTH)] = ins[r][256:320]


def unpack(me, parts):
    return pl.pallas_call(
        unpack_kernel,
        in_specs=[scalars()] + [pl.BlockSpec(memory_space=pltpu.VMEM)] * CTX,
        out_shape=[
            jax.ShapeDtypeStruct((1, KEY_ROWS, CTX * WIDTH), BF16),
            jax.ShapeDtypeStruct((1, KEY_ROWS, CTX * WIDTH), BF16),
            jax.ShapeDtypeStruct((1, ROWS, CTX * WIDTH), BF16),
        ],
        compiler_params=params(),
        cost_estimate=cost(0, 4 << 20),
    )(me, *parts)


def weight_kernel(me_ref, *refs):
    ins, (own_ref, other_ref, o_ref, a_ref, b_ref, acc_ref, out_ref) = refs[:4], refs[4:]
    step = pl.program_id(0)
    for j in range(4):

        @pl.when(step == j)
        def _():
            for x in range(4):
                a_ref[:, 128 * x:128 * (x + 1)] = ins[j][x].reshape(384, 128)

    for x in range(4):
        b_ref[x, me_ref[MC]] = own_ref[x, 0]
        b_ref[x, 1 - me_ref[MC]] = other_ref[x, 0]
    product = jnp.dot(a_ref[...], b_ref[...].reshape(512, 1536), preferred_element_type=F32)

    @pl.when(step == 0)
    def _():
        acc_ref[...] = product

    @pl.when(step > 0)
    def _():
        acc_ref[...] += product

    @pl.when(step == 3)
    def _():
        for zh in range(4):
            for yz in range(8):
                row = zh * 96 + yz * 12
                for j in range(12):
                    out_ref[yz * 4 + zh, 12 * j:12 * j + 12, :] = acc_ref[row:row + 12, 128 * j:128 * (j + 1)]
        o_ref[...] = out_ref[...].astype(BF16)


def weight_partial(me, parts, own, other):
    shared = pl.BlockSpec((4, 1, ROWS, 1536), lambda j, me: (0, lax.rem(me[MY] + 4 - j, 4), 0, 0))
    return pl.pallas_call(
        weight_kernel,
        grid_spec=pltpu.PrefetchScalarGridSpec(
            num_scalar_prefetch=1,
            grid=(4,),
            in_specs=[pl.BlockSpec((4, 4, 96, 128), lambda j, me: (0, 0, 0, 0))] * 4 + [shared, shared],
            out_specs=pl.BlockSpec((32, 144, 128), lambda j, me: (0, 0, 0)),
            scratch_shapes=[
                pltpu.VMEM((384, 512), BF16),
                pltpu.VMEM((4, 2, ROWS, 1536), BF16),
                pltpu.VMEM((384, 1536), F32),
                pltpu.VMEM((32, 144, 128), F32),
            ],
        ),
        out_shape=jax.ShapeDtypeStruct((32, 144, 128), BF16),
        compiler_params=params(),
        cost_estimate=cost(2 * 384 * 2048 * 1536, 9 << 20),
    )(me, *parts, own, other)


def total_kernel(r_ref, o_ref, sum_ref):
    for y in range(4):
        total = r_ref[8 * y].astype(F32)
        for z in range(1, 8):
            total = total + r_ref[8 * y + z].astype(F32)
        sum_ref[y] = total
        for j in range(12):
            lane = (12 * y + j) * 128
            o_ref[:, lane:lane + 128] = sum_ref[y, 12 * j:12 * j + 12, :]


def weight_total(received):
    return pl.pallas_call(
        total_kernel,
        out_shape=jax.ShapeDtypeStruct((12, 6144), F32),
        scratch_shapes=[pltpu.VMEM((4, 144, 128), F32)],
        compiler_params=params(),
        cost_estimate=cost(1 << 20, 2 << 20),
    )(received)


def exchange(blocks, axes):
    return lax.all_to_all(blocks, axes, split_axis=0, concat_axis=0, tiled=True)


def around(blocks, axis):
    rounds = [[(i, (i + k) % 4) for i in range(4)] for k in range(4)]
    return [blocks[0]] + [lax.ppermute(blocks[k], axis, rounds[k]) for k in (1, 2, 3)]


def to_owners(blocks):
    moved = list(blocks)
    for r in (1, 2, 3, 6, 7, 4, 5):
        pairs = [(z * 2 + c, (z + r // 2) % 4 * 2 + (c + r) % 2) for z in range(4) for c in range(2)]
        moved[r] = lax.ppermute(blocks[r], ("zh", "core"), pairs)
    return moved


def tie(value, *others):
    return lax.optimization_barrier((value,) + others)[0]


def on_device(queries, keys, values, tan_q, tan_k, tan_v, attn_cot, out_cot):
    me = jnp.stack([lax.axis_index(a) for a in ("x", "y", "zh", "core")]).astype(jnp.int32)
    *own, sib = pack_ahead(me, keys, values, queries)
    own = around(own, "zh")
    sib = lax.ppermute(sib, "core", SWAP)
    cot = exchange(spread_cot(tie(out_cot, sib)), ("x", "y")).reshape(4, 4, ROWS, 1536)
    tangents = pack(*(tie(a, sib) for a in (tan_k, tan_v, tan_q, attn_cot)))
    sib = around([sib[dz] for dz in range(4)], "zh")
    packed = [block for pair in zip(own, sib) for block in pair]
    packed[0] = tie(packed[0], tangents, cot)

    att = around(forward(me, packed), "zh")
    tangents = exchange(tie(tangents, *att), ("zh", "core"))
    other = lax.ppermute(cot, "core", SWAP)
    att = around(turn(me, att), "x")
    att = around([join(me, MX, att)] * 4, "y")
    partial = weight_partial(me, att, cot, other)
    tangents = tie(tangents, partial)
    weight = weight_total(exchange(partial, ("y", "zl", "zh")))

    grads = to_owners(backward(me, packed, tangents))
    grads[0] = tie(grads[0], weight)
    grad_k, grad_v, grad_q = unpack(me, grads)
    return grad_q, grad_k, grad_v, weight


def solution(mesh):
    fine = Mesh(mesh.devices.reshape(4, 4, 2, 4, 2), ("x", "y", "zl", "zh", "core"))
    clip, token = ("x", "y", "zl"), ("zh", "core")
    placed = P(clip, token, None)
    return jax.shard_map(
        on_device,
        mesh=fine,
        in_specs=(placed,) * 8,
        out_specs=(placed, placed, placed, P(token + clip, None)),
        check_vma=False,
    )
```

```python
import functools

import jax
import jax.numpy as jnp
from jax import lax
from jax.experimental import pallas as pl
from jax.experimental.pallas import tpu as pltpu
from jax.sharding import Mesh, PartitionSpec as P

E = 128
HEADS = 3
WIDTH = HEADS * E
CTX = 8
ROWS = 64
KEY_ROWS = 128
FACTOR = E ** -0.5
LOG2E = 1.4426950408889634
F32 = jnp.float32
BF16 = jnp.bfloat16
MX, MY, MZ, MC = range(4)
SWAP = [(0, 1), (1, 0)]
VMEM_LIMIT = 56 * 1024 * 1024

NT = (((1,), (1,)), ((), ()))
TN = (((0,), (0,)), ((), ()))


def params():
    return pltpu.CompilerParams(vmem_limit_bytes=VMEM_LIMIT)


def cost(flops, moved, exps=0):
    return pl.CostEstimate(flops=flops, bytes_accessed=moved, transcendentals=exps)


def scalars():
    return pl.BlockSpec(memory_space=pltpu.SMEM)


def pack_kernel(*refs):
    o_ref = refs[-1]
    row = 0
    for ref in refs[:-1]:
        n = ref.shape[1]
        for d in range(CTX):
            o_ref[d, row:row + n] = ref[0, :, d * WIDTH:(d + 1) * WIDTH]
        row += n


def pack(*arrays):
    rows = sum(a.shape[1] for a in arrays)
    return pl.pallas_call(
        pack_kernel,
        out_shape=jax.ShapeDtypeStruct((CTX, rows, WIDTH), BF16),
        compiler_params=params(),
        cost_estimate=cost(0, 4 * rows * CTX * WIDTH),
    )(*arrays)


def split_cot_kernel(me_ref, c_ref, *outs):
    for j in range(4):
        lane = lax.rem(me_ref[MY] + j, 4) * 1536
        outs[j][...] = c_ref[0, :, pl.ds(pl.multiple_of(lane, 128), 1536)]


def split_cot(me, out_cot):
    return pl.pallas_call(
        split_cot_kernel,
        in_specs=[scalars(), pl.BlockSpec(memory_space=pltpu.VMEM)],
        out_shape=[jax.ShapeDtypeStruct((ROWS, 1536), BF16)] * 4,
        compiler_params=params(),
        cost_estimate=cost(0, 1600000),
    )(me, out_cot)


def join_kernel(axis, me_ref, *refs):
    o_ref = refs[-1]
    for j in range(4):
        o_ref[lax.rem(me_ref[axis] + 4 - j, 4)] = refs[j][...]


def join(me, axis, parts):
    return pl.pallas_call(
        functools.partial(join_kernel, axis),
        in_specs=[scalars()] + [pl.BlockSpec(memory_space=pltpu.VMEM)] * 4,
        out_shape=jax.ShapeDtypeStruct((4,) + parts[0].shape, BF16),
        compiler_params=params(),
        cost_estimate=cost(0, 16 * parts[0].size),
    )(me, *parts)


def turn_kernel(me_ref, *refs):
    ins, outs = refs[:4], refs[4:]
    for k in range(4):
        zh = lax.rem(me_ref[MZ] + 4 - k, 4)
        for j in range(4):
            outs[j][zh] = ins[k][lax.rem(me_ref[MX] + j, 4)]


def turn(me, parts):
    return pl.pallas_call(
        turn_kernel,
        in_specs=[scalars()] + [pl.BlockSpec(memory_space=pltpu.VMEM)] * 4,
        out_shape=[jax.ShapeDtypeStruct((4, 96, 128), BF16)] * 4,
        compiler_params=params(),
        cost_estimate=cost(0, 800000),
    )(me, *parts)


def probabilities(q, k):
    s = lax.dot_general(q, k, NT, preferred_element_type=F32)
    highest = jnp.max(s, axis=-1, keepdims=True)
    w = jnp.exp2((s - highest) * (FACTOR * LOG2E))
    return w * (1.0 / jnp.sum(w, axis=-1, keepdims=True))


def forward_kernel(me_ref, k_ref, v_ref, q_ref, *refs):
    outs, all_ref = refs[:4], refs[4]
    for h in range(HEADS):
        lanes = slice(h * E, (h + 1) * E)
        k = k_ref[:, :, lanes].reshape(1024, E)
        v = v_ref[:, :, lanes].reshape(1024, E)
        for part in range(2):
            q = q_ref[4 * part:4 * part + 4, :, lanes].reshape(256, E)
            p = probabilities(q, k).astype(BF16)
            o = jnp.dot(p, v, preferred_element_type=F32)
            turned = o.T.astype(BF16)
            f = 0
            while f < E:
                g = h * E + f
                slot, row = g // 96, g % 96
                n = min(E - f, 96 - row)
                for t in range(2):
                    all_ref[part * 2 + t, slot, row:row + n, :] = turned[f:f + n, t * 128:(t + 1) * 128]
                f += n
    for j in range(4):
        outs[j][...] = all_ref[lax.rem(me_ref[MZ] + j, 4)]


def forward(me, packed):
    return pl.pallas_call(
        forward_kernel,
        grid=(1,),
        in_specs=[
            scalars(),
            pl.BlockSpec((CTX, 128, WIDTH), lambda i: (0, 0, 0)),
            pl.BlockSpec((CTX, 128, WIDTH), lambda i: (0, 1, 0)),
            pl.BlockSpec((CTX, 64, WIDTH), lambda i: (0, 4, 0)),
        ],
        out_specs=[pl.BlockSpec((4, 96, 128), lambda i: (0, 0, 0))] * 4,
        out_shape=[jax.ShapeDtypeStruct((4, 96, 128), BF16)] * 4,
        scratch_shapes=[pltpu.VMEM((4, 4, 96, 128), BF16)],
        compiler_params=params(),
        cost_estimate=cost(3 * 2 * 2 * 512 * 1024 * 128, 3 << 20, 3 * 512 * 1024),
    )(me, packed, packed, packed)


def backward_kernel(me_ref, k_ref, v_ref, q_ref, t_ref, *refs):
    outs, (o_ref, gk_ref, gv_ref) = refs[:CTX], refs[CTX:]
    k = k_ref[...].reshape(1024, E)
    v = v_ref[...].reshape(1024, E)
    tk = t_ref[:, 0:128].reshape(1024, E)
    tv = t_ref[:, 128:256].reshape(1024, E)
    tk_k = jnp.concatenate([tk, k], axis=1)
    v_tv = jnp.concatenate([v, tv], axis=1)
    for part in range(2):
        own = slice(4 * part, 4 * part + 4)
        q = q_ref[own].reshape(256, E)
        tq = t_ref[own, 256:320].reshape(256, E)
        cot = t_ref[own, 320:384].reshape(256, E).astype(F32)
        p = probabilities(q, k)
        p_low = p.astype(BF16)
        mixed = p * lax.dot_general(
            jnp.concatenate([q, tq], axis=1), tk_k, NT, preferred_element_type=F32
        )
        rows = jnp.sum(mixed, axis=-1, keepdims=True)
        both = jnp.dot(p_low, v_tv, preferred_element_type=F32)
        out_full = both[:, :E]
        tangent = both[:, E:] + FACTOR * (
            jnp.dot(mixed.astype(BF16), v, preferred_element_type=F32) - rows * out_full
        )
        grad_out = (cot + tangent).astype(BF16)
        delta = jnp.sum(
            grad_out.astype(F32) * out_full.astype(BF16).astype(F32), axis=-1, keepdims=True
        )
        grad_probs = lax.dot_general(grad_out, v, NT, preferred_element_type=F32)
        grad_scores = (p * (grad_probs - delta)).astype(BF16)
        grad_q = jnp.dot(grad_scores, k, preferred_element_type=F32) * FACTOR
        o_ref[own, 256:320] = grad_q.astype(BF16).reshape(4, ROWS, E)
        grad_k = lax.dot_general(q, grad_scores, TN, preferred_element_type=F32)
        grad_v = lax.dot_general(grad_out, p_low, TN, preferred_element_type=F32)
        if part == 0:
            gk_ref[...] = grad_k
            gv_ref[...] = grad_v
        else:
            grad_k = gk_ref[...] + grad_k
            grad_v = gv_ref[...] + grad_v
            o_ref[:, 0:128] = (grad_k * FACTOR).T.astype(BF16).reshape(CTX, 128, E)
            o_ref[:, 128:256] = grad_v.T.astype(BF16).reshape(CTX, 128, E)
    for r in range(CTX):
        outs[r][...] = o_ref[partner(me_ref, r // 2, r % 2)]


def partner(me_ref, ahead, other):
    return lax.rem(me_ref[MZ] + ahead, 4) * 2 + lax.rem(me_ref[MC] + other, 2)


def backward(me, packed, tangents):
    return pl.pallas_call(
        backward_kernel,
        grid=(HEADS,),
        in_specs=[
            scalars(),
            pl.BlockSpec((CTX, 128, E), lambda h: (0, 0, h)),
            pl.BlockSpec((CTX, 128, E), lambda h: (0, 1, h)),
            pl.BlockSpec((CTX, 64, E), lambda h: (0, 4, h)),
            pl.BlockSpec((CTX, 384, E), lambda h: (0, 0, h)),
        ],
        out_specs=[pl.BlockSpec((320, E), lambda h: (0, h))] * CTX,
        out_shape=[jax.ShapeDtypeStruct((320, WIDTH), BF16)] * CTX,
        scratch_shapes=[
            pltpu.VMEM((CTX, 320, E), BF16),
            pltpu.VMEM((E, 1024), F32),
            pltpu.VMEM((E, 1024), F32),
        ],
        compiler_params=params(),
        cost_estimate=cost(3 * 10 * 2 * 512 * 1024 * 128, 6 << 20, 3 * 512 * 1024),
    )(me, packed, packed, packed, tangents)


def unpack_kernel(me_ref, *refs):
    ins, (gk_ref, gv_ref, gq_ref) = refs[:CTX], refs[CTX:]
    for r in range(CTX):
        lane = pl.multiple_of(partner(me_ref, 4 - r // 2, r % 2) * WIDTH, 128)
        gk_ref[0, :, pl.ds(lane, WIDTH)] = ins[r][0:128]
        gv_ref[0, :, pl.ds(lane, WIDTH)] = ins[r][128:256]
        gq_ref[0, :, pl.ds(lane, WIDTH)] = ins[r][256:320]


def unpack(me, parts):
    return pl.pallas_call(
        unpack_kernel,
        in_specs=[scalars()] + [pl.BlockSpec(memory_space=pltpu.VMEM)] * CTX,
        out_shape=[
            jax.ShapeDtypeStruct((1, KEY_ROWS, CTX * WIDTH), BF16),
            jax.ShapeDtypeStruct((1, KEY_ROWS, CTX * WIDTH), BF16),
            jax.ShapeDtypeStruct((1, ROWS, CTX * WIDTH), BF16),
        ],
        compiler_params=params(),
        cost_estimate=cost(0, 4 << 20),
    )(me, *parts)


def weight_kernel(me_ref, *refs):
    ins, own, other, (o_ref, a_ref, b_ref, acc_ref, out_ref) = refs[:4], refs[4:8], refs[8:12], refs[12:]
    step = pl.program_id(0)
    for j in range(4):

        @pl.when(step == j)
        def _():
            for x in range(4):
                block = ins[j][lax.rem(me_ref[MX] + 4 - x, 4)]
                a_ref[:, 128 * x:128 * (x + 1)] = block.reshape(384, 128)

    for x in range(4):
        b_ref[x, me_ref[MC]] = own[x][0]
        b_ref[x, 1 - me_ref[MC]] = other[x][0]
    product = jnp.dot(a_ref[...], b_ref[...].reshape(512, 1536), preferred_element_type=F32)

    @pl.when(step == 0)
    def _():
        acc_ref[...] = product

    @pl.when(step > 0)
    def _():
        acc_ref[...] += product

    @pl.when(step == 3)
    def _():
        for zh in range(4):
            for yz in range(8):
                row = zh * 96 + yz * 12
                for j in range(12):
                    out_ref[yz * 4 + zh, 12 * j:12 * j + 12, :] = acc_ref[row:row + 12, 128 * j:128 * (j + 1)]
        o_ref[...] = out_ref[...].astype(BF16)


def weight_partial(me, parts, own, other):
    shared = pl.BlockSpec((1, ROWS, 1536), lambda j, me: (lax.rem(me[MY] + 4 - j, 4), 0, 0))
    return pl.pallas_call(
        weight_kernel,
        grid_spec=pltpu.PrefetchScalarGridSpec(
            num_scalar_prefetch=1,
            grid=(4,),
            in_specs=[pl.BlockSpec((4, 4, 96, 128), lambda j, me: (0, 0, 0, 0))] * 4 + [shared] * 8,
            out_specs=pl.BlockSpec((32, 144, 128), lambda j, me: (0, 0, 0)),
            scratch_shapes=[
                pltpu.VMEM((384, 512), BF16),
                pltpu.VMEM((4, 2, ROWS, 1536), BF16),
                pltpu.VMEM((384, 1536), F32),
                pltpu.VMEM((32, 144, 128), F32),
            ],
        ),
        out_shape=jax.ShapeDtypeStruct((32, 144, 128), BF16),
        compiler_params=params(),
        cost_estimate=cost(2 * 384 * 2048 * 1536, 9 << 20),
    )(me, *parts, *own, *other)


def total_kernel(r_ref, o_ref, sum_ref):
    for y in range(4):
        total = r_ref[8 * y].astype(F32)
        for z in range(1, 8):
            total = total + r_ref[8 * y + z].astype(F32)
        sum_ref[y] = total
        for j in range(12):
            lane = (12 * y + j) * 128
            o_ref[:, lane:lane + 128] = sum_ref[y, 12 * j:12 * j + 12, :]


def weight_total(received):
    return pl.pallas_call(
        total_kernel,
        out_shape=jax.ShapeDtypeStruct((12, 6144), F32),
        scratch_shapes=[pltpu.VMEM((4, 144, 128), F32)],
        compiler_params=params(),
        cost_estimate=cost(1 << 20, 2 << 20),
    )(received)


def exchange(blocks, axes):
    return lax.all_to_all(blocks, axes, split_axis=0, concat_axis=0, tiled=True)


def around(blocks, axis):
    rounds = [[(i, (i + k) % 4) for i in range(4)] for k in range(4)]
    return [blocks[0]] + [lax.ppermute(blocks[k], axis, rounds[k]) for k in (1, 2, 3)]


def to_owners(blocks):
    moved = [blocks[0]]
    for r in range(1, CTX):
        pairs = [(z * 2 + c, (z + r // 2) % 4 * 2 + (c + r) % 2) for z in range(4) for c in range(2)]
        moved.append(lax.ppermute(blocks[r], ("zh", "core"), pairs))
    return moved


def tie(value, *others):
    return lax.optimization_barrier((value,) + others)[0]


def on_device(queries, keys, values, tan_q, tan_k, tan_v, attn_cot, out_cot):
    me = jnp.stack([lax.axis_index(a) for a in ("x", "y", "zh", "core")]).astype(jnp.int32)
    packed = pack(keys, values, queries)
    tangents = pack(*(tie(a, packed) for a in (tan_k, tan_v, tan_q, attn_cot)))
    cot = join(me, MY, around(split_cot(me, tie(out_cot, packed)), "y"))
    cot = around([cot] * 4, "x")
    packed = tie(exchange(packed, ("zh", "core")), tangents, cot[1])

    att = around(forward(me, packed), "zh")
    tangents = exchange(tie(tangents, *att, *cot), ("zh", "core"))
    other = [lax.ppermute(c, "core", SWAP) for c in cot]
    att[0] = tie(att[0], *other)
    att = around(turn(me, att), "x")
    att = around([join(me, MX, att)] * 4, "y")
    partial = weight_partial(me, att, cot, other)
    tangents = tie(tangents, partial)
    weight = weight_total(exchange(partial, ("y", "zl", "zh")))

    grads = to_owners(backward(me, packed, tangents))
    grads[0] = tie(grads[0], weight)
    grad_k, grad_v, grad_q = unpack(me, grads)
    return grad_q, grad_k, grad_v, weight


def solution(mesh):
    fine = Mesh(mesh.devices.reshape(4, 4, 2, 4, 2), ("x", "y", "zl", "zh", "core"))
    clip, token = ("x", "y", "zl"), ("zh", "core")
    placed = P(clip, token, None)
    return jax.shard_map(
        on_device,
        mesh=fine,
        in_specs=(placed,) * 8,
        out_specs=(placed, placed, placed, P(token + clip, None)),
        check_vma=False,
    )
```

```python
import functools

import jax
import jax.numpy as jnp
from jax import lax
from jax.experimental import pallas as pl
from jax.experimental.pallas import tpu as pltpu
from jax.sharding import Mesh, PartitionSpec as P

E = 128
HEADS = 3
WIDTH = HEADS * E
CTX = 8
ROWS = 64
KEY_ROWS = 128
FACTOR = E ** -0.5
LOG2E = 1.4426950408889634
F32 = jnp.float32
BF16 = jnp.bfloat16
MX, MY, MZ, MC = range(4)
SWAP = [(0, 1), (1, 0)]
VMEM_LIMIT = 56 * 1024 * 1024

NT = (((1,), (1,)), ((), ()))
TN = (((0,), (0,)), ((), ()))


def params():
    return pltpu.CompilerParams(vmem_limit_bytes=VMEM_LIMIT)


def cost(flops, moved, exps=0):
    return pl.CostEstimate(flops=flops, bytes_accessed=moved, transcendentals=exps)


def scalars():
    return pl.BlockSpec(memory_space=pltpu.SMEM)


def pack_kernel(*refs):
    o_ref = refs[-1]
    row = 0
    for ref in refs[:-1]:
        n = ref.shape[1]
        for d in range(CTX):
            o_ref[d, row:row + n] = ref[0, :, d * WIDTH:(d + 1) * WIDTH]
        row += n


def pack(*arrays):
    rows = sum(a.shape[1] for a in arrays)
    return pl.pallas_call(
        pack_kernel,
        out_shape=jax.ShapeDtypeStruct((CTX, rows, WIDTH), BF16),
        compiler_params=params(),
        cost_estimate=cost(0, 4 * rows * CTX * WIDTH),
    )(*arrays)


def split_cot_kernel(me_ref, c_ref, *outs):
    for j in range(4):
        lane = lax.rem(me_ref[MY] + j, 4) * 1536
        outs[j][...] = c_ref[0, :, pl.ds(pl.multiple_of(lane, 128), 1536)]


def split_cot(me, out_cot):
    return pl.pallas_call(
        split_cot_kernel,
        in_specs=[scalars(), pl.BlockSpec(memory_space=pltpu.VMEM)],
        out_shape=[jax.ShapeDtypeStruct((ROWS, 1536), BF16)] * 4,
        compiler_params=params(),
        cost_estimate=cost(0, 1600000),
    )(me, out_cot)


def join_kernel(axis, me_ref, *refs):
    o_ref = refs[-1]
    for j in range(4):
        o_ref[lax.rem(me_ref[axis] + 4 - j, 4)] = refs[j][...]


def join(me, axis, parts):
    return pl.pallas_call(
        functools.partial(join_kernel, axis),
        in_specs=[scalars()] + [pl.BlockSpec(memory_space=pltpu.VMEM)] * 4,
        out_shape=jax.ShapeDtypeStruct((4,) + parts[0].shape, BF16),
        compiler_params=params(),
        cost_estimate=cost(0, 16 * parts[0].size),
    )(me, *parts)


def turn_kernel(me_ref, *refs):
    ins, outs = refs[:4], refs[4:]
    for k in range(4):
        zh = lax.rem(me_ref[MZ] + 4 - k, 4)
        for j in range(4):
            outs[j][zh] = ins[k][lax.rem(me_ref[MX] + j, 4)]


def turn(me, parts):
    return pl.pallas_call(
        turn_kernel,
        in_specs=[scalars()] + [pl.BlockSpec(memory_space=pltpu.VMEM)] * 4,
        out_shape=[jax.ShapeDtypeStruct((4, 96, 128), BF16)] * 4,
        compiler_params=params(),
        cost_estimate=cost(0, 800000),
    )(me, *parts)


def probabilities(q, k):
    s = lax.dot_general(q, k, NT, preferred_element_type=F32)
    highest = jnp.max(s, axis=-1, keepdims=True)
    w = jnp.exp2((s - highest) * (FACTOR * LOG2E))
    return w * (1.0 / jnp.sum(w, axis=-1, keepdims=True))


def forward_kernel(me_ref, k_ref, v_ref, q_ref, *refs):
    outs, all_ref = refs[:4], refs[4]
    for h in range(HEADS):
        lanes = slice(h * E, (h + 1) * E)
        k = k_ref[:, :, lanes].reshape(1024, E)
        v = v_ref[:, :, lanes].reshape(1024, E)
        for part in range(2):
            q = q_ref[4 * part:4 * part + 4, :, lanes].reshape(256, E)
            p = probabilities(q, k).astype(BF16)
            o = jnp.dot(p, v, preferred_element_type=F32)
            turned = o.T.astype(BF16)
            f = 0
            while f < E:
                g = h * E + f
                slot, row = g // 96, g % 96
                n = min(E - f, 96 - row)
                for t in range(2):
                    all_ref[part * 2 + t, slot, row:row + n, :] = turned[f:f + n, t * 128:(t + 1) * 128]
                f += n
    for j in range(4):
        outs[j][...] = all_ref[lax.rem(me_ref[MZ] + j, 4)]


def forward(me, packed):
    return pl.pallas_call(
        forward_kernel,
        grid=(1,),
        in_specs=[
            scalars(),
            pl.BlockSpec((CTX, 128, WIDTH), lambda i: (0, 0, 0)),
            pl.BlockSpec((CTX, 128, WIDTH), lambda i: (0, 1, 0)),
            pl.BlockSpec((CTX, 64, WIDTH), lambda i: (0, 4, 0)),
        ],
        out_specs=[pl.BlockSpec((4, 96, 128), lambda i: (0, 0, 0))] * 4,
        out_shape=[jax.ShapeDtypeStruct((4, 96, 128), BF16)] * 4,
        scratch_shapes=[pltpu.VMEM((4, 4, 96, 128), BF16)],
        compiler_params=params(),
        cost_estimate=cost(3 * 2 * 2 * 512 * 1024 * 128, 3 << 20, 3 * 512 * 1024),
    )(me, packed, packed, packed)


def backward_kernel(me_ref, k_ref, v_ref, q_ref, t_ref, *refs):
    outs, (sib_ref, o_ref, gk_ref, gv_ref) = refs[:4], refs[4:]
    k = k_ref[...].reshape(1024, E)
    v = v_ref[...].reshape(1024, E)
    tk = t_ref[:, 0:128].reshape(1024, E)
    tv = t_ref[:, 128:256].reshape(1024, E)
    tk_k = jnp.concatenate([tk, k], axis=1)
    v_tv = jnp.concatenate([v, tv], axis=1)
    for part in range(2):
        own = slice(4 * part, 4 * part + 4)
        q = q_ref[own].reshape(256, E)
        tq = t_ref[own, 256:320].reshape(256, E)
        cot = t_ref[own, 320:384].reshape(256, E).astype(F32)
        p = probabilities(q, k)
        p_low = p.astype(BF16)
        mixed = p * lax.dot_general(
            jnp.concatenate([q, tq], axis=1), tk_k, NT, preferred_element_type=F32
        )
        rows = jnp.sum(mixed, axis=-1, keepdims=True)
        both = jnp.dot(p_low, v_tv, preferred_element_type=F32)
        out_full = both[:, :E]
        tangent = both[:, E:] + FACTOR * (
            jnp.dot(mixed.astype(BF16), v, preferred_element_type=F32) - rows * out_full
        )
        grad_out = (cot + tangent).astype(BF16)
        delta = jnp.sum(
            grad_out.astype(F32) * out_full.astype(BF16).astype(F32), axis=-1, keepdims=True
        )
        grad_probs = lax.dot_general(grad_out, v, NT, preferred_element_type=F32)
        grad_scores = (p * (grad_probs - delta)).astype(BF16)
        grad_q = jnp.dot(grad_scores, k, preferred_element_type=F32) * FACTOR
        o_ref[own, 256:320] = grad_q.astype(BF16).reshape(4, ROWS, E)
        grad_k = lax.dot_general(q, grad_scores, TN, preferred_element_type=F32)
        grad_v = lax.dot_general(grad_out, p_low, TN, preferred_element_type=F32)
        if part == 0:
            gk_ref[...] = grad_k
            gv_ref[...] = grad_v
        else:
            grad_k = gk_ref[...] + grad_k
            grad_v = gv_ref[...] + grad_v
            o_ref[:, 0:128] = (grad_k * FACTOR).T.astype(BF16).reshape(CTX, 128, E)
            o_ref[:, 128:256] = grad_v.T.astype(BF16).reshape(CTX, 128, E)
    for dz in range(4):
        outs[dz][...] = o_ref[partner(me_ref, dz, 0)]
        sib_ref[dz] = o_ref[partner(me_ref, dz, 1)]


def partner(me_ref, ahead, other):
    return lax.rem(me_ref[MZ] + ahead, 4) * 2 + lax.rem(me_ref[MC] + other, 2)


def backward(me, packed, tangents):
    return pl.pallas_call(
        backward_kernel,
        grid=(HEADS,),
        in_specs=[
            scalars(),
            pl.BlockSpec((CTX, 128, E), lambda h: (0, 0, h)),
            pl.BlockSpec((CTX, 128, E), lambda h: (0, 1, h)),
            pl.BlockSpec((CTX, 64, E), lambda h: (0, 4, h)),
            pl.BlockSpec((CTX, 384, E), lambda h: (0, 0, h)),
        ],
        out_specs=[pl.BlockSpec((320, E), lambda h: (0, h))] * 4
        + [pl.BlockSpec((4, 320, E), lambda h: (0, 0, h))],
        out_shape=[jax.ShapeDtypeStruct((320, WIDTH), BF16)] * 4
        + [jax.ShapeDtypeStruct((4, 320, WIDTH), BF16)],
        scratch_shapes=[
            pltpu.VMEM((CTX, 320, E), BF16),
            pltpu.VMEM((E, 1024), F32),
            pltpu.VMEM((E, 1024), F32),
        ],
        compiler_params=params(),
        cost_estimate=cost(3 * 10 * 2 * 512 * 1024 * 128, 6 << 20, 3 * 512 * 1024),
    )(me, packed, packed, packed, tangents)


def merge_kernel(own1_ref, own3_ref, sib_ref, near_ref, far_ref, sib0_ref, sib2_ref):
    near_ref[0] = own1_ref[...]
    near_ref[1] = sib_ref[1]
    far_ref[0] = own3_ref[...]
    far_ref[1] = sib_ref[3]
    sib0_ref[...] = sib_ref[0]
    sib2_ref[...] = sib_ref[2]


def merge(own, sib):
    return pl.pallas_call(
        merge_kernel,
        out_shape=[jax.ShapeDtypeStruct((2, 320, WIDTH), BF16)] * 2
        + [jax.ShapeDtypeStruct((320, WIDTH), BF16)] * 2,
        compiler_params=params(),
        cost_estimate=cost(0, 4 << 20),
    )(own[1], own[3], sib)


def unpack_kernel(me_ref, own0_ref, sib0_ref, near_ref, own2_ref, sib2_ref, far_ref, gk_ref, gv_ref, gq_ref):
    blocks = (own0_ref, sib0_ref, near_ref.at[0], near_ref.at[1], own2_ref, sib2_ref, far_ref.at[0], far_ref.at[1])
    for r in range(CTX):
        lane = pl.multiple_of(partner(me_ref, 4 - r // 2, r % 2) * WIDTH, 128)
        gk_ref[0, :, pl.ds(lane, WIDTH)] = blocks[r][0:128]
        gv_ref[0, :, pl.ds(lane, WIDTH)] = blocks[r][128:256]
        gq_ref[0, :, pl.ds(lane, WIDTH)] = blocks[r][256:320]


def unpack(me, parts):
    return pl.pallas_call(
        unpack_kernel,
        in_specs=[scalars()] + [pl.BlockSpec(memory_space=pltpu.VMEM)] * 6,
        out_shape=[
            jax.ShapeDtypeStruct((1, KEY_ROWS, CTX * WIDTH), BF16),
            jax.ShapeDtypeStruct((1, KEY_ROWS, CTX * WIDTH), BF16),
            jax.ShapeDtypeStruct((1, ROWS, CTX * WIDTH), BF16),
        ],
        compiler_params=params(),
        cost_estimate=cost(0, 4 << 20),
    )(me, *parts)


def ahead(block):
    return lax.ppermute(block, "zh", [(i, (i + 1) % 4) for i in range(4)])


def behind(block):
    return lax.ppermute(block, "zh", [(i, (i + 3) % 4) for i in range(4)])


def weight_kernel(me_ref, *refs):
    ins, own, other, (o_ref, a_ref, b_ref, acc_ref, out_ref) = refs[:4], refs[4:8], refs[8:12], refs[12:]
    step = pl.program_id(0)
    for j in range(4):

        @pl.when(step == j)
        def _():
            for x in range(4):
                block = ins[j][lax.rem(me_ref[MX] + 4 - x, 4)]
                a_ref[:, 128 * x:128 * (x + 1)] = block.reshape(384, 128)

    for x in range(4):
        b_ref[x, me_ref[MC]] = own[x][0]
        b_ref[x, 1 - me_ref[MC]] = other[x][0]
    product = jnp.dot(a_ref[...], b_ref[...].reshape(512, 1536), preferred_element_type=F32)

    @pl.when(step == 0)
    def _():
        acc_ref[...] = product

    @pl.when(step > 0)
    def _():
        acc_ref[...] += product

    @pl.when(step == 3)
    def _():
        for zh in range(4):
            for yz in range(8):
                row = zh * 96 + yz * 12
                slot = (yz % 2 * 4 + zh) * 4 + yz // 2
                for j in range(12):
                    out_ref[slot, 12 * j:12 * j + 12, :] = acc_ref[row:row + 12, 128 * j:128 * (j + 1)]
        o_ref[...] = out_ref[...].astype(BF16)


def weight_partial(me, parts, own, other):
    shared = pl.BlockSpec((1, ROWS, 1536), lambda j, me: (lax.rem(me[MY] + 4 - j, 4), 0, 0))
    return pl.pallas_call(
        weight_kernel,
        grid_spec=pltpu.PrefetchScalarGridSpec(
            num_scalar_prefetch=1,
            grid=(4,),
            in_specs=[pl.BlockSpec((4, 4, 96, 128), lambda j, me: (0, 0, 0, 0))] * 4 + [shared] * 8,
            out_specs=pl.BlockSpec((32, 144, 128), lambda j, me: (0, 0, 0)),
            scratch_shapes=[
                pltpu.VMEM((384, 512), BF16),
                pltpu.VMEM((4, 2, ROWS, 1536), BF16),
                pltpu.VMEM((384, 1536), F32),
                pltpu.VMEM((32, 144, 128), F32),
            ],
        ),
        out_shape=jax.ShapeDtypeStruct((32, 144, 128), BF16),
        compiler_params=params(),
        cost_estimate=cost(2 * 384 * 2048 * 1536, 9 << 20),
    )(me, *parts, *own, *other)


def layers_kernel(r_ref, o_ref):
    for y in range(4):
        total = r_ref[0, y].astype(F32)
        for z in range(1, 8):
            total = total + r_ref[z, y].astype(F32)
        o_ref[y] = total


def layers_total(received):
    return pl.pallas_call(
        layers_kernel,
        out_shape=jax.ShapeDtypeStruct((4, 144, 128), F32),
        compiler_params=params(),
        cost_estimate=cost(1 << 20, 2 << 20),
    )(received)


def rows_kernel(r_ref, o_ref):
    for y in range(4):
        for j in range(12):
            lane = (12 * y + j) * 128
            o_ref[:, lane:lane + 128] = r_ref[y, 12 * j:12 * j + 12, :]


def weight_rows(received):
    return pl.pallas_call(
        rows_kernel,
        out_shape=jax.ShapeDtypeStruct((12, 6144), F32),
        compiler_params=params(),
        cost_estimate=cost(0, 1 << 20),
    )(received)


def exchange(blocks, axes):
    return lax.all_to_all(blocks, axes, split_axis=0, concat_axis=0, tiled=True)


def around(blocks, axis):
    rounds = [[(i, (i + k) % 4) for i in range(4)] for k in range(4)]
    return [blocks[0]] + [lax.ppermute(blocks[k], axis, rounds[k]) for k in (1, 2, 3)]


def tie(value, *others):
    return lax.optimization_barrier((value,) + others)[0]


def on_device(queries, keys, values, tan_q, tan_k, tan_v, attn_cot, out_cot):
    me = jnp.stack([lax.axis_index(a) for a in ("x", "y", "zh", "core")]).astype(jnp.int32)
    packed = pack(keys, values, queries)
    tangents = pack(*(tie(a, packed) for a in (tan_k, tan_v, tan_q, attn_cot)))
    cot = join(me, MY, around(split_cot(me, tie(out_cot, packed)), "y"))
    cot = around([cot] * 4, "x")
    packed = tie(exchange(packed, ("zh", "core")), tangents, cot[1])

    att = around(forward(me, packed), "zh")
    tangents = exchange(tie(tangents, *att, *cot), ("zh", "core"))
    other = [lax.ppermute(c, "core", SWAP) for c in cot]
    att[0] = tie(att[0], *other)
    att = around(turn(me, att), "x")
    att = around([join(me, MX, att)] * 4, "y")
    partial = weight_partial(me, att, cot, other)
    tangents = tie(tangents, partial)
    partial = exchange(partial.reshape(8, 4, 144, 128), ("zl", "zh"))
    weight = weight_rows(exchange(layers_total(partial), "y"))

    *own, sib = backward(me, packed, tangents)
    own2 = ahead(own[2])
    near, far, sib0, sib2 = merge(own, lax.ppermute(sib, "core", SWAP))
    sib2 = behind(sib2)
    near, far = ahead(near), behind(far)
    own2, sib2 = ahead(own2), behind(sib2)
    own0 = tie(own[0], weight)
    grad_k, grad_v, grad_q = unpack(me, (own0, sib0, near, own2, sib2, far))
    return grad_q, grad_k, grad_v, weight


def solution(mesh):
    fine = Mesh(mesh.devices.reshape(4, 4, 2, 4, 2), ("x", "y", "zl", "zh", "core"))
    clip, token = ("x", "y", "zl"), ("zh", "core")
    placed = P(clip, token, None)
    return jax.shard_map(
        on_device,
        mesh=fine,
        in_specs=(placed,) * 8,
        out_specs=(placed, placed, placed, P(token + clip, None)),
        check_vma=False,
    )
```
